32 devices in a mesh: grp: 2 (over y), tm: 4 (over z), fibre: 2 (over x), rep: 2 (over core).
Axes of the slice: x: 2, y: 2, z: 4, core: 2. Of those that a mesh axis runs over, the one named last changes fastest.
Arguments:
- records: bfloat16 [512, 256], P(('grp', 'fibre'), ('tm', 'rep')), parts along dimension 0, may hold values from -6 to 6
- taps: float32 [256, 64], P('fibre'), may hold values from -4 to 4
- obs_matrix: float32 [256, 256], P('fibre'), may hold values from -0.375 to 0.375
- noise_prec: float32 [16, 256], P(('grp', 'tm', 'rep'), 'fibre'), parts along dimension 0, may hold values from 0.05 to 0.5, as said below
- proc_prec: float32 [256], replicated, may hold values from 100 to 100000
- mode_decay: float32 [128], replicated, may hold values from 0.97 to 1
- mode_angle: float32 [128], replicated, may hold values from -3.140625 to 3.140625
Outputs:
- filtered: float32 [16, 256], P(('grp', 'tm', 'rep')), parts along dimension 0
- smoothed: float32 [16, 256], P(('grp', 'tm', 'rep')), parts along dimension 0
The draws below stay inside these ranges and needn't reach their ends.
There are 2 independent parts, one for each index of `grp`. The reference program is written for one: setup_inputs(seed, part) draws one part's arguments, and reference() takes and returns one part's arrays. A program takes and returns all parts, laid end to end along the dimension named above; an argument that names none is the same for every part. Nothing has to cross between parts.
Inputs may be any that keep to these rules, and one draw needn't show every extreme that they name: `noise_prec`: positive precisions.
All inputs are finite; a program needn't handle non-finite values.
Results may differ from the reference program's by a relative error of at most 0.0003.
Values may be sent and summed in bfloat16 or wider, within the bound.
A program may use at most 128 MiB of HBM per device.

```python
import math
import jax
import jax.numpy as jnp
from jax import lax

NS = 256
MODES = 128
NCH = 256
TAPS = 64
HOP = 32
RECURSION_COUNT = 8
SAMPLES = 256


def draw_noise_prec(key, part):
    base_key = jax.random.fold_in(key, 11)
    first_key = jax.random.fold_in(base_key, 0)
    anchor_location = jnp.exp(jax.random.uniform(first_key, (RECURSION_COUNT, NCH), jnp.float32, math.log(0.05), math.log(0.5)))
    return anchor_location


def steps_of(stream_key, extent, pieces, low, high):
    loudness, own = 1.0, jax.random.fold_in(stream_key, 6)
    for axis_at, shards_of in pieces:
        steps = jnp.exp(jax.random.uniform(jax.random.fold_in(own, axis_at), (shards_of,), jnp.float32, low / len(pieces), high / len(pieces)))
        loudness = loudness * jnp.repeat(steps, extent[axis_at] // shards_of).reshape([-1 if axis == axis_at else 1 for axis in range(len(extent))])
    return loudness


def centred(rng, extent, scale, limit, shards=(), kind=jnp.bfloat16):
    entries = scale * jax.random.normal(rng, extent, jnp.float32)
    if shards:
        entries = entries * steps_of(rng, extent, shards, -0.22, 0.18)
    return jnp.clip(entries, -limit, limit).astype(kind)


def setup_inputs(seed: int = 0, part: int = 0) -> dict:
    seeds = jax.random.split(jax.random.key(seed), 8)
    own_keys = jax.random.split(jax.random.fold_in(seeds[7], part), 8)
    records = centred(own_keys[0], (NCH, SAMPLES), 1.0, 6.0, ((0, 2), (1, 8)))
    taps = centred(seeds[1], (NCH, TAPS), 1.0, 4.0, ((0, 2),), jnp.float32)
    obs_matrix = centred(seeds[2], (NCH, NS), NS ** -0.5, 0.375, ((0, 2),), jnp.float32)
    noise_prec = draw_noise_prec(jax.random.fold_in(jax.random.fold_in(seeds[7], part), 71), part)
    proc_prec = jnp.clip(jnp.exp(jax.random.uniform(seeds[4], (NS,), jnp.float32, math.log(100.0), math.log(100000.0))), 100.0, 100000.0)
    mode_decay = jnp.clip(jnp.exp(jax.random.uniform(seeds[5], (MODES,), jnp.float32, math.log(0.97), math.log(1.0))), 0.97, 1.0)
    mode_angle = jnp.clip(jax.random.uniform(seeds[6], (MODES,), jnp.float32, -3.140625, 3.140625), -3.140625, 3.140625)
    return {"records": records, "taps": taps, "obs_matrix": obs_matrix, "noise_prec": noise_prec, "proc_prec": proc_prec, "mode_decay": mode_decay, "mode_angle": mode_angle}


def product(leading_portion, right_part):
    return jnp.dot(leading_portion.astype(jnp.float32), right_part.astype(jnp.float32), precision=lax.Precision.HIGHEST, preferred_element_type=jnp.float32)

def inverse_spd(matrix, identity):
    factor = jnp.linalg.cholesky(matrix)
    inverse = jax.scipy.linalg.solve_triangular(factor, identity, lower=True)
    return product(inverse.T, inverse)

def reference(records, taps, obs_matrix, noise_prec, proc_prec, mode_decay, mode_angle):
    slack_allowance = TAPS - HOP
    padded = jnp.concatenate([jnp.zeros((NCH, slack_allowance), jnp.float32), records.astype(jnp.float32)], axis=1)
    starts = HOP * jnp.arange(RECURSION_COUNT, dtype=jnp.int32)
    offsets = (starts[:, None] + jnp.arange(TAPS, dtype=jnp.int32)[None, :]).astype(jnp.int32)
    frames = padded[:, offsets]
    measured = jnp.sum(frames * taps[:, None, :], axis=2).T
    cos_part = mode_decay * jnp.cos(mode_angle)
    sin_part = mode_decay * jnp.sin(mode_angle)
    transition = jnp.block([[jnp.diag(cos_part), -jnp.diag(sin_part)], [jnp.diag(sin_part), jnp.diag(cos_part)]])
    noise_cov = jnp.diag(1.0 / proc_prec)
    identity = jnp.eye(NS, dtype=jnp.float32)

    def forward(carried, inputs):
        centre, spread = carried
        weights, numeric_quantities, opening = inputs
        pred_centre = jnp.where(opening, jnp.zeros((NS,), jnp.float32), product(transition, centre))
        pred_spread = jnp.where(opening, identity, product(product(transition, spread), transition.T) + noise_cov)
        fisher = product(obs_matrix.T * weights[None, :], obs_matrix)
        fisher_vector = product(weights * numeric_quantities, obs_matrix)
        pred_prec = inverse_spd(pred_spread, identity)
        new_spread = inverse_spd(pred_prec + fisher, identity)
        new_centre = product(new_spread, product(pred_prec, pred_centre) + fisher_vector)
        return ((new_centre, new_spread), (new_centre, new_spread))
    openings = jnp.arange(RECURSION_COUNT, dtype=jnp.int32) == 0
    start_state = (jnp.zeros((NS,), jnp.float32), identity)
    _, (filtered, spreads) = lax.scan(forward, start_state, (noise_prec, measured, openings))

    def backward(later, inputs):
        centre, spread = inputs
        pred_spread = product(product(transition, spread), transition.T) + noise_cov
        factor = jnp.linalg.cholesky(pred_spread)
        half_solve = jax.scipy.linalg.solve_triangular(factor, product(transition, spread), lower=True)
        gain_t = jax.scipy.linalg.solve_triangular(factor, half_solve, lower=True, trans=1)
        smooth = centre + product(gain_t.T, later - product(transition, centre))
        return (smooth, smooth)
    _, earlier = lax.scan(backward, filtered[-1], (filtered[:-1], spreads[:-1]), reverse=True)
    smoothed = jnp.concatenate([earlier, filtered[-1:]], axis=0)
    return (filtered, smoothed)
```

```python
import functools

import jax
import jax.numpy as jnp
from jax import lax
from jax.experimental import pallas as pl
from jax.experimental.pallas import tpu as pltpu
from jax.sharding import PartitionSpec as P

F32 = jnp.float32
BF16 = jnp.bfloat16
MESH = pl.DeviceIdType.MESH
HIGHEST = lax.Precision.HIGHEST


def split(value):
    high = value.astype(BF16)
    return high, (value - high.astype(F32)).astype(BF16)


def gather_kernel(
    counts, records_ref, taps_ref, obs_ref, noise_ref, prec_ref, decay_ref, angle_ref,
    high_ref, low_ref, high_t_ref, low_t_ref, data_ref, weight_ref, table_ref, pick_ref,
    message, notes, shapes, send_sem, recv_sem, obs_send, obs_recv,
):
    n_tm, n_fibre, n_rep = counts
    total = n_tm * n_fibre * n_rep
    steps = n_tm * n_rep
    channels = obs_ref.shape[0]
    t, f, r = lax.axis_index("tm"), lax.axis_index("fibre"), lax.axis_index("rep")
    position = t * n_rep + r
    me = position * n_fibre + f

    def place(index):
        at, fibre = index // n_fibre, index % n_fibre
        return at, fibre, {"tm": at // n_rep, "fibre": fibre, "rep": at % n_rep}

    barrier = pltpu.get_barrier_semaphore()

    @pl.loop(1, total)
    def _(i):
        pl.semaphore_signal(barrier, inc=1, device_id=place((me + i) % total)[2], device_id_type=MESH)

    block = records_ref[...].astype(F32)
    hop = block.shape[1]
    taps = taps_ref[...]
    ones = jnp.ones((8, hop), F32)
    contract = (((1,), (1,)), ((), ()))
    now = lax.dot_general(ones, block * taps[:, hop:], contract, precision=HIGHEST, preferred_element_type=F32)
    later = lax.dot_general(ones, block * taps[:, :hop], contract, precision=HIGHEST, preferred_element_type=F32)
    message[0:1, :] = now[0:1]
    message[1:2, :] = later[0:1]
    message[2:3, :] = noise_ref[...]
    message[3:8, :] = jnp.zeros((5, channels), F32)

    pl.semaphore_wait(barrier, total - 1)

    obs_copies = []
    for i in range(1, n_fibre):
        copy = pltpu.make_async_remote_copy(
            src_ref=obs_ref, dst_ref=shapes.at[f], send_sem=obs_send.at[i], recv_sem=obs_recv.at[i],
            device_id={"tm": t, "fibre": (f + i) % n_fibre, "rep": r}, device_id_type=MESH,
        )
        copy.start()
        obs_copies.append(copy)

    def note(at, fibre, target, index_send, index_recv):
        return pltpu.make_async_remote_copy(
            src_ref=message, dst_ref=notes.at[fibre, at], send_sem=send_sem.at[index_send],
            recv_sem=recv_sem.at[index_recv], device_id=target, device_id_type=MESH,
        )

    @pl.loop(1, total)
    def _(i):
        other = (me + i) % total
        note(position, f, place(other)[2], other, me).start()

    notes[f, position] = message[...]
    shapes[f] = obs_ref[...]

    row = lax.broadcasted_iota(jnp.int32, (steps, 1), 0)
    power = row.astype(F32)
    turned = power * angle_ref[...]
    grown = jnp.exp(power * jnp.log(decay_ref[...]))
    cosine, sine = jnp.cos(turned), jnp.sin(turned)
    half = angle_ref.shape[1]
    noise_u = jnp.where(row == 0, 1.0, 1.0 / prec_ref[:, :half])
    noise_v = jnp.where(row == 0, 1.0, 1.0 / prec_ref[:, half:])
    back = 1.0 / (grown * grown)
    table_ref[0] = grown * cosine
    table_ref[1] = grown * sine
    table_ref[2] = back * (cosine * cosine * noise_u + sine * sine * noise_v)
    table_ref[3] = back * (cosine * sine * (noise_v - noise_u))
    table_ref[4] = back * (sine * sine * noise_u + cosine * cosine * noise_v)
    pick_ref[...] = jnp.broadcast_to((row == position).astype(F32), pick_ref.shape)

    @pl.loop(1, total)
    def _(i):
        other = (me + i) % total
        at, fibre, where = place(other)
        arrival = note(at, fibre, where, other, other)
        arrival.wait_recv()
        arrival.wait_send()

    lane = row <= position
    for fibre in range(n_fibre):
        here = slice(fibre * channels, (fibre + 1) * channels)
        for at in range(steps):
            data_ref[at : at + 1, here] = notes[fibre, at, 0:1, :]
            weight_ref[at : at + 1, here] = notes[fibre, at, 2:3, :]
            if at:
                data_ref[at : at + 1, here] += notes[fibre, at - 1, 1:2, :]
    root = jnp.sqrt(weight_ref[0:steps, :])
    measured = data_ref[0:steps, :]
    masked = jnp.where(lane, root, 0.0)
    weight_ref[0:steps, :] = masked
    weight_ref[steps:, :] = root
    data_ref[0:steps, :] = masked * measured
    data_ref[steps:, :] = root * measured

    for copy in obs_copies:
        copy.wait()
    for fibre in range(n_fibre):
        here = slice(fibre * channels, (fibre + 1) * channels)
        whole = shapes[fibre]
        high_ref[here, :], low_ref[here, :] = split(whole)
        high_t_ref[:, here], low_t_ref[:, here] = split(whole.T)


def running_sum(value, row, reverse):
    steps = value.shape[0]
    stride = 1
    while stride < steps:
        if reverse:
            value = value + jnp.where(row < steps - stride, pltpu.roll(value, steps - stride, 0), 0.0)
        else:
            value = value + jnp.where(row >= stride, pltpu.roll(value, stride, 0), 0.0)
        stride *= 2
    return value


CHUNK = 4
FIRST = 12
MOST = 4000
TARGET = 1e-10


def solve_kernel(high_ref, low_ref, high_t_ref, low_t_ref, data_ref, weight_ref, table_ref, pick_ref,
                 filtered_ref, smoothed_ref):
    steps = pick_ref.shape[0]
    half = table_ref.shape[2]
    row = lax.broadcasted_iota(jnp.int32, (steps, half), 0)
    weight = weight_ref[...]
    data = data_ref[...]
    both = (slice(0, steps), slice(steps, 2 * steps))

    def times(value, high, low):
        top, rest = split(value)
        n = value.shape[0]
        wide = jnp.dot(jnp.concatenate([top, rest], axis=0), high[...], preferred_element_type=F32)
        return wide[:n] + wide[n:] + jnp.dot(top, low[...], preferred_element_type=F32)

    def states(value):
        seen = times(weight * value, high_ref, low_ref)
        moved = []
        for rows in both:
            u, v = seen[rows, :half], seen[rows, half:]
            cosine, sine = table_ref[0], table_ref[1]
            u, v = cosine * u + sine * v, cosine * v - sine * u
            u, v = running_sum(u, row, True), running_sum(v, row, True)
            u, v = table_ref[2] * u + table_ref[3] * v, table_ref[3] * u + table_ref[4] * v
            u, v = running_sum(u, row, False), running_sum(v, row, False)
            u, v = cosine * u - sine * v, sine * u + cosine * v
            moved.append(jnp.concatenate([u, v], axis=1))
        return jnp.concatenate(moved, axis=0)

    def apply(value):
        return value + weight * times(states(value), high_t_ref, low_t_ref)

    def inner(a, b):
        product = a * b
        return [
            jnp.sum(jnp.sum(product[rows], axis=0, keepdims=True), axis=1, keepdims=True) for rows in both
        ]

    def scaled(factors, value):
        return jnp.concatenate([k * value[rows] for k, rows in zip(factors, both)], axis=0)

    def ratio(a, b):
        good = b > 0
        return jnp.where(good, a / jnp.where(good, b, 1.0), 0.0)

    def step(carry):
        answer, left, along, image, before, size = carry
        mapped = apply(left)
        gamma = inner(left, left)
        delta = inner(left, mapped)
        beta = [ratio(g, o) for g, o in zip(gamma, before)]
        size = [d - b * b * s for d, b, s in zip(delta, beta, size)]
        alpha = [ratio(g, s) for g, s in zip(gamma, size)]
        along = left + scaled(beta, along)
        image = mapped + scaled(beta, image)
        answer = answer + scaled(alpha, along)
        left = left - scaled(alpha, image)
        return answer, left, along, image, gamma, size

    zeros = jnp.zeros_like(data)
    none = [jnp.zeros((1, 1), F32)] * 2
    carry = (zeros, data, zeros, zeros, none, none)
    goal = [TARGET * g for g in inner(data, data)]

    def behind(left):
        excess = [g - o for g, o in zip(inner(left, left), goal)]
        return jnp.max(jnp.maximum(excess[0], excess[1]))

    for _ in range(FIRST):
        carry = step(carry)

    def body(state):
        count, carry, _ = state
        for _ in range(CHUNK):
            carry = step(carry)
        return count + CHUNK, carry, behind(carry[1])

    _, carry, _ = lax.while_loop(
        lambda state: (state[2] > 0) & (state[0] < MOST), body, (jnp.int32(0), carry, behind(carry[1]))
    )
    result = states(carry[0])
    pick = pick_ref[...]
    filtered_ref[...] = jnp.sum(pick * result[both[0]], axis=0, keepdims=True)
    smoothed_ref[...] = jnp.sum(pick * result[both[1]], axis=0, keepdims=True)


def solution(mesh):
    counts = tuple(mesh.shape[name] for name in ("tm", "fibre", "rep"))
    steps = counts[0] * counts[2]

    def on_device(records, taps, obs_matrix, noise_prec, proc_prec, mode_decay, mode_angle):
        own, state = obs_matrix.shape
        channels = own * counts[1]
        total = counts[1] * steps
        vmem = pl.BlockSpec(memory_space=pltpu.VMEM)
        shape = jax.ShapeDtypeStruct
        parts = pl.pallas_call(
            functools.partial(gather_kernel, counts),
            out_shape=(
                shape((channels, state), BF16), shape((channels, state), BF16),
                shape((state, channels), BF16), shape((state, channels), BF16),
                shape((2 * steps, channels), F32), shape((2 * steps, channels), F32),
                shape((5, steps, state // 2), F32), shape((steps, state), F32),
            ),
            in_specs=[vmem] * 7,
            out_specs=(vmem,) * 8,
            scratch_shapes=[
                pltpu.VMEM((8, own), F32),
                pltpu.VMEM((counts[1], steps, 8, own), F32),
                pltpu.VMEM((counts[1], own, state), F32),
                pltpu.SemaphoreType.DMA((total,)),
                pltpu.SemaphoreType.DMA((total,)),
                pltpu.SemaphoreType.DMA((counts[1],)),
                pltpu.SemaphoreType.DMA((counts[1],)),
            ],
            compiler_params=pltpu.CompilerParams(
                collective_id=0, has_side_effects=True, vmem_limit_bytes=32 * 2**20
            ),
        )(records, taps, obs_matrix, noise_prec, proc_prec[None], mode_decay[None], mode_angle[None])
        return pl.pallas_call(
            solve_kernel,
            out_shape=(shape((1, state), F32), shape((1, state), F32)),
            in_specs=[vmem] * 8,
            out_specs=(vmem, vmem),
            compiler_params=pltpu.CompilerParams(vmem_limit_bytes=32 * 2**20),
        )(*parts)

    return jax.shard_map(
        on_device,
        mesh=mesh,
        in_specs=(
            P(("grp", "fibre"), ("tm", "rep")),
            P("fibre", None),
            P("fibre", None),
            P(("grp", "tm", "rep"), "fibre"),
            P(),
            P(),
            P(),
        ),
        out_specs=(P(("grp", "tm", "rep"), None), P(("grp", "tm", "rep"), None)),
        check_vma=False,
    )
```

```python
import functools

import jax
import jax.numpy as jnp
from jax import lax
from jax.experimental import pallas as pl
from jax.experimental.pallas import tpu as pltpu
from jax.sharding import PartitionSpec as P

F32 = jnp.float32
BF16 = jnp.bfloat16
MESH = pl.DeviceIdType.MESH
HIGHEST = lax.Precision.HIGHEST


def split(value):
    high = value.astype(BF16)
    return high, (value - high.astype(F32)).astype(BF16)


def gather_kernel(
    counts, records_ref, taps_ref, obs_ref, noise_ref, prec_ref, decay_ref, angle_ref,
    high_ref, low_ref, high_t_ref, low_t_ref, data_ref, weight_ref, table_ref, pick_ref, shapes,
    records_in, taps_in, noise_in, prec_in, decay_in, angle_in,
    message, notes, local_sem, send_sem, recv_sem, obs_send, obs_recv, die_send, die_recv,
):
    n_tm, n_fibre, n_rep = counts
    total = n_tm * n_fibre * n_rep
    steps = n_tm * n_rep
    channels = obs_ref.shape[0]
    t, f, r = lax.axis_index("tm"), lax.axis_index("fibre"), lax.axis_index("rep")
    position = t * n_rep + r
    me = f * steps + position

    def place(index):
        fibre, at = index // steps, index % steps
        return at, fibre, {"tm": at // n_rep, "fibre": fibre, "rep": at % n_rep}

    barrier = pltpu.get_barrier_semaphore()

    def greet(i):
        pl.semaphore_signal(barrier, inc=1, device_id=place((me + i) % total)[2], device_id_type=MESH)

    for i in range(1, n_fibre):
        greet(i * steps)
    for i in range(1, n_fibre + 1):
        @pl.loop((i - 1) * steps + 1, i * steps)
        def _(j):
            greet(j)

    loads = [
        pltpu.make_async_copy(source, target, local_sem.at[number])
        for number, (source, target) in enumerate((
            (records_ref, records_in), (taps_ref, taps_in), (noise_ref, noise_in), (prec_ref, prec_in),
            (decay_ref, decay_in), (angle_ref, angle_in), (obs_ref, shapes.at[f]),
        ))
    ]
    for load in loads:
        load.start()
    for load in loads[:3]:
        load.wait()

    block = records_in[...].astype(F32)
    hop = block.shape[0]
    message[0:1, :] = jnp.sum(block * taps_in[hop:, :], axis=0, keepdims=True)
    message[1:2, :] = jnp.sum(block * taps_in[:hop, :], axis=0, keepdims=True)
    message[2:3, :] = noise_in[...]
    message[3:8, :] = jnp.zeros((5, channels), F32)

    pl.semaphore_wait(barrier, total - 1)

    share = channels // n_rep
    mine = pl.ds(pl.multiple_of(r * share, share), share)
    obs_copies = []
    for i in range(1, n_fibre):
        copy = pltpu.make_async_remote_copy(
            src_ref=obs_ref.at[mine], dst_ref=shapes.at[f, mine], send_sem=obs_send.at[i], recv_sem=obs_recv.at[i],
            device_id={"tm": t, "fibre": (f + i) % n_fibre, "rep": r}, device_id_type=MESH,
        )
        copy.start()
        obs_copies.append(copy)

    def note(at, fibre, target, index_send, index_recv):
        return pltpu.make_async_remote_copy(
            src_ref=message, dst_ref=notes.at[fibre, at], send_sem=send_sem.at[index_send],
            recv_sem=recv_sem.at[index_recv], device_id=target, device_id_type=MESH,
        )

    @pl.loop(1, total)
    def _(i):
        other = (me + i) % total
        note(position, f, place(other)[2], other, me).start()

    notes[f, position] = message[...]
    for load in loads[3:]:
        load.wait()

    row = lax.broadcasted_iota(jnp.int32, (steps, 1), 0)
    power = row.astype(F32)
    turned = power * angle_in[...]
    grown = jnp.exp(power * jnp.log(decay_in[...]))
    cosine, sine = jnp.cos(turned), jnp.sin(turned)
    half = angle_in.shape[1]
    noise_u = jnp.where(row == 0, 1.0, 1.0 / prec_in[:, :half])
    noise_v = jnp.where(row == 0, 1.0, 1.0 / prec_in[:, half:])
    back = 1.0 / (grown * grown)
    table_ref[0] = grown * cosine
    table_ref[1] = grown * sine
    table_ref[2] = back * (cosine * cosine * noise_u + sine * sine * noise_v)
    table_ref[3] = back * (cosine * sine * (noise_v - noise_u))
    table_ref[4] = back * (sine * sine * noise_u + cosine * cosine * noise_v)
    pick_ref[...] = jnp.broadcast_to((row == position).astype(F32), pick_ref.shape)

    def keep(fibre):
        here = pl.ds(pl.multiple_of(fibre * channels, channels), channels)
        whole = shapes[fibre]
        high_ref[here, :], low_ref[here, :] = split(whole)
        high_t_ref[:, here], low_t_ref[:, here] = split(whole.T)

    keep(f)

    passed = []
    for i in range(1, n_fibre):
        obs_copies[i - 1].wait_recv()
        source = (f + n_fibre - i) % n_fibre
        for j in range(1, n_rep):
            number = (i - 1) * n_rep + j
            copy = pltpu.make_async_remote_copy(
                src_ref=shapes.at[source, mine], dst_ref=shapes.at[source, mine],
                send_sem=die_send.at[number], recv_sem=die_recv.at[number],
                device_id={"tm": t, "fibre": f, "rep": (r + j) % n_rep}, device_id_type=MESH,
            )
            copy.start()
            passed.append(copy)

    @pl.loop(1, total)
    def _(i):
        other = (me + i) % total
        at, fibre, where = place(other)
        arrival = note(at, fibre, where, other, other)
        arrival.wait_recv()
        arrival.wait_send()

    lane = row <= position
    for fibre in range(n_fibre):
        here = slice(fibre * channels, (fibre + 1) * channels)
        for at in range(steps):
            data_ref[at : at + 1, here] = notes[fibre, at, 0:1, :]
            weight_ref[at : at + 1, here] = notes[fibre, at, 2:3, :]
            if at:
                data_ref[at : at + 1, here] += notes[fibre, at - 1, 1:2, :]
    root = jnp.sqrt(weight_ref[0:steps, :])
    measured = data_ref[0:steps, :]
    masked = jnp.where(lane, root, 0.0)
    weight_ref[0:steps, :] = masked
    weight_ref[steps:, :] = root
    data_ref[0:steps, :] = masked * measured
    data_ref[steps:, :] = root * measured

    for copy in passed:
        copy.wait()
    for copy in obs_copies:
        copy.wait_send()
    for i in range(1, n_fibre):
        keep((f + i) % n_fibre)


def running_sum(value, row, reverse):
    steps = value.shape[0]
    stride = 1
    while stride < steps:
        if reverse:
            value = value + jnp.where(row < steps - stride, pltpu.roll(value, steps - stride, 0), 0.0)
        else:
            value = value + jnp.where(row >= stride, pltpu.roll(value, stride, 0), 0.0)
        stride *= 2
    return value


FIRST = 10
CHUNK = 4
MOST = 4000
TARGET = 2.5e-9
STRONG = 64.0


def solve_kernel(high_ref, low_ref, high_t_ref, low_t_ref, data_ref, weight_ref, table_ref, pick_ref, shapes_ref,
                 filtered_ref, smoothed_ref):
    steps = pick_ref.shape[0]
    half = table_ref.shape[2]
    channels = shapes_ref.shape[1]
    row = lax.broadcasted_iota(jnp.int32, (steps, half), 0)
    weight = weight_ref[...]
    data = data_ref[...]
    both = (slice(0, steps), slice(steps, 2 * steps))

    def times(value, high, low):
        top, rest = split(value)
        n = value.shape[0]
        wide = jnp.dot(jnp.concatenate([top, rest], axis=0), high[...], preferred_element_type=F32)
        return wide[:n] + wide[n:] + jnp.dot(top, low[...], preferred_element_type=F32)

    def carried(seen):
        moved = []
        for rows in both:
            u, v = seen[rows, :half], seen[rows, half:]
            cosine, sine = table_ref[0], table_ref[1]
            u, v = cosine * u + sine * v, cosine * v - sine * u
            u, v = running_sum(u, row, True), running_sum(v, row, True)
            u, v = table_ref[2] * u + table_ref[3] * v, table_ref[3] * u + table_ref[4] * v
            u, v = running_sum(u, row, False), running_sum(v, row, False)
            u, v = cosine * u - sine * v, sine * u + cosine * v
            moved.append(jnp.concatenate([u, v], axis=1))
        return jnp.concatenate(moved, axis=0)

    def states(value):
        return carried(times(weight * value, high_ref, low_ref))

    def apply(value):
        return value + weight * times(states(value), high_t_ref, low_t_ref)

    def states_full(value):
        scaled_value = weight * value
        seen = jnp.zeros((2 * steps, 2 * half), F32)
        for fibre in range(shapes_ref.shape[0]):
            own = scaled_value[:, fibre * channels : (fibre + 1) * channels]
            seen += jnp.dot(own, shapes_ref[fibre], precision=HIGHEST, preferred_element_type=F32)
        return carried(seen)

    def apply_full(value):
        moved = states_full(value)
        back = [
            lax.dot_general(moved, shapes_ref[fibre], (((1,), (1,)), ((), ())), precision=HIGHEST,
                            preferred_element_type=F32)
            for fibre in range(shapes_ref.shape[0])
        ]
        return value + weight * jnp.concatenate(back, axis=1)

    def inner(a, b):
        product = a * b
        return [
            jnp.sum(jnp.sum(product[rows], axis=0, keepdims=True), axis=1, keepdims=True) for rows in both
        ]

    def scaled(factors, value):
        return jnp.concatenate([k * value[rows] for k, rows in zip(factors, both)], axis=0)

    def ratio(a, b):
        good = b > 0
        return jnp.where(good, a / jnp.where(good, b, 1.0), 0.0)

    def store(result):
        pick = pick_ref[...]
        filtered_ref[...] = jnp.sum(pick * result[both[0]], axis=0, keepdims=True)
        smoothed_ref[...] = jnp.sum(pick * result[both[1]], axis=0, keepdims=True)

    zeros = jnp.zeros_like(data)
    none = [jnp.zeros((1, 1), F32)] * 2
    answer, left, along, image, second = zeros, data, zeros, zeros, zeros
    before, size, largest = none, none, none
    goal = None
    mapped = apply(data)
    for number in range(FIRST):
        gamma = inner(left, left)
        delta = inner(left, mapped)
        if number == 0:
            goal = [TARGET * g for g in gamma]
        beta = [ratio(g, o) for g, o in zip(gamma, before)]
        size = [d - b * b * s for d, b, s in zip(delta, beta, size)]
        alpha = [ratio(g, s) for g, s in zip(gamma, size)]
        largest = [jnp.maximum(l, ratio(d, g)) for l, d, g in zip(largest, delta, gamma)]
        before = gamma
        along = left + scaled(beta, along)
        image = mapped + scaled(beta, image)
        answer = answer + scaled(alpha, along)
        left = left - scaled(alpha, image)
        if number + 1 < FIRST:
            second = apply(mapped) + scaled(beta, second)
            mapped = mapped - scaled(alpha, second)
    excess = [jnp.maximum(g - o, l - STRONG) for g, o, l in zip(inner(left, left), goal, largest)]
    store(states(answer))

    def behind(left):
        return jnp.max(jnp.maximum(*[g - o for g, o in zip(inner(left, left), goal)]))

    @pl.when(jnp.max(jnp.maximum(*excess)) > 0)
    def _():
        def step(carry):
            answer, left, along, image, before, size = carry
            mapped = apply_full(left)
            gamma = inner(left, left)
            delta = inner(left, mapped)
            beta = [ratio(g, o) for g, o in zip(gamma, before)]
            size = [d - b * b * s for d, b, s in zip(delta, beta, size)]
            alpha = [ratio(g, s) for g, s in zip(gamma, size)]
            along = left + scaled(beta, along)
            image = mapped + scaled(beta, image)
            return answer + scaled(alpha, along), left - scaled(alpha, image), along, image, gamma, size

        def burst(state):
            count, carry, _ = state
            for _ in range(CHUNK):
                carry = step(carry)
            return count + CHUNK, carry, behind(carry[1])

        def going(state):
            return (state[2] > 0) & (state[0] < MOST)

        start = data - apply_full(answer)
        carry = (answer, start, zeros, zeros, none, none)
        _, carry, _ = lax.while_loop(going, burst, (jnp.int32(0), carry, behind(start)))
        store(states_full(carry[0]))


def solution(mesh):
    counts = tuple(mesh.shape[name] for name in ("tm", "fibre", "rep"))
    steps = counts[0] * counts[2]

    def on_device(records, taps, obs_matrix, noise_prec, proc_prec, mode_decay, mode_angle):
        own, state = obs_matrix.shape
        channels = own * counts[1]
        total = counts[1] * steps
        vmem = pl.BlockSpec(memory_space=pltpu.VMEM)
        hbm = pl.BlockSpec(memory_space=pltpu.HBM)
        shape = jax.ShapeDtypeStruct
        hop, width = records.shape[1], taps.shape[1]
        parts = pl.pallas_call(
            functools.partial(gather_kernel, counts),
            out_shape=(
                shape((channels, state), BF16), shape((channels, state), BF16),
                shape((state, channels), BF16), shape((state, channels), BF16),
                shape((2 * steps, channels), F32), shape((2 * steps, channels), F32),
                shape((5, steps, state // 2), F32), shape((steps, state), F32),
                shape((counts[1], own, state), F32),
            ),
            in_specs=[hbm] * 7,
            out_specs=(vmem,) * 9,
            scratch_shapes=[
                pltpu.VMEM((hop, own), BF16),
                pltpu.VMEM((width, own), F32),
                pltpu.VMEM((1, own), F32),
                pltpu.VMEM((1, state), F32),
                pltpu.VMEM((1, state // 2), F32),
                pltpu.VMEM((1, state // 2), F32),
                pltpu.VMEM((8, own), F32),
                pltpu.VMEM((counts[1], steps, 8, own), F32),
                pltpu.SemaphoreType.DMA((7,)),
                pltpu.SemaphoreType.DMA((total,)),
                pltpu.SemaphoreType.DMA((total,)),
                pltpu.SemaphoreType.DMA((counts[1],)),
                pltpu.SemaphoreType.DMA((counts[1],)),
                pltpu.SemaphoreType.DMA((counts[1] * counts[2],)),
                pltpu.SemaphoreType.DMA((counts[1] * counts[2],)),
            ],
            compiler_params=pltpu.CompilerParams(
                collective_id=0, has_side_effects=True, vmem_limit_bytes=32 * 2**20
            ),
        )(*(
            pltpu.with_memory_space_constraint(value, pltpu.HBM)
            for value in (
                records.T, taps.T, obs_matrix, noise_prec, proc_prec[None], mode_decay[None], mode_angle[None]
            )
        ))
        return pl.pallas_call(
            solve_kernel,
            out_shape=(shape((1, state), F32), shape((1, state), F32)),
            in_specs=[vmem] * 9,
            out_specs=(vmem, vmem),
            compiler_params=pltpu.CompilerParams(vmem_limit_bytes=32 * 2**20),
        )(*parts)

    return jax.shard_map(
        on_device,
        mesh=mesh,
        in_specs=(
            P(("grp", "fibre"), ("tm", "rep")),
            P("fibre", None),
            P("fibre", None),
            P(("grp", "tm", "rep"), "fibre"),
            P(),
            P(),
            P(),
        ),
        out_specs=(P(("grp", "tm", "rep"), None), P(("grp", "tm", "rep"), None)),
        check_vma=False,
    )
```

```python
import functools

import jax
import jax.numpy as jnp
from jax import lax
from jax.experimental import pallas as pl
from jax.experimental.pallas import tpu as pltpu
from jax.sharding import PartitionSpec as P

F32 = jnp.float32
BF16 = jnp.bfloat16
MESH = pl.DeviceIdType.MESH
HIGHEST = lax.Precision.HIGHEST


def split(value):
    high = value.astype(BF16)
    return high, (value - high.astype(F32)).astype(BF16)


def gather_kernel(
    counts, records_ref, taps_ref, obs_ref, noise_ref, prec_ref, decay_ref, angle_ref,
    high_ref, low_ref, high_t_ref, low_t_ref, data_ref, weight_ref, table_ref, pick_ref, shapes,
    records_in, taps_in, noise_in, prec_in, decay_in, angle_in,
    notes, local_sem, send_sem, recv_sem, plane_send, plane_recv, obs_send, obs_recv, die_send, die_recv,
):
    n_tm, n_fibre, n_rep = counts
    steps = n_tm * n_rep
    channels = obs_ref.shape[0]
    t, f, r = lax.axis_index("tm"), lax.axis_index("fibre"), lax.axis_index("rep")
    position = t * n_rep + r
    column = [{"tm": (t + i) % n_tm, "fibre": f, "rep": r} for i in range(1, n_tm)]
    plane = [
        {"tm": t, "fibre": (f + i) % n_fibre, "rep": (r + j) % n_rep}
        for i in range(n_fibre) for j in range(n_rep) if i or j
    ]
    barrier = pltpu.get_barrier_semaphore()
    for target in column + plane:
        pl.semaphore_signal(barrier, inc=1, device_id=target, device_id_type=MESH)

    loads = [
        pltpu.make_async_copy(source, target, local_sem.at[number])
        for number, (source, target) in enumerate((
            (records_ref, records_in), (taps_ref, taps_in), (noise_ref, noise_in), (prec_ref, prec_in),
            (decay_ref, decay_in), (angle_ref, angle_in), (obs_ref, shapes.at[f]),
        ))
    ]
    for load in loads:
        load.start()
    for load in loads[:3]:
        load.wait()

    block = records_in[...].astype(F32)
    hop = block.shape[0]
    mine_note = notes.at[f, r, t]
    mine_note[:, 0:channels] = jnp.sum(block * taps_in[hop:, :], axis=0, keepdims=True)
    mine_note[:, channels : 2 * channels] = jnp.sum(block * taps_in[:hop, :], axis=0, keepdims=True)
    mine_note[:, 2 * channels :] = noise_in[...]

    pl.semaphore_wait(barrier, len(column) + len(plane))

    share = channels // n_rep
    mine = pl.ds(pl.multiple_of(r * share, share), share)
    obs_copies = []
    for i in range(1, n_fibre):
        copy = pltpu.make_async_remote_copy(
            src_ref=obs_ref.at[mine], dst_ref=shapes.at[f, mine], send_sem=obs_send.at[i], recv_sem=obs_recv.at[i],
            device_id={"tm": t, "fibre": (f + i) % n_fibre, "rep": r}, device_id_type=MESH,
        )
        copy.start()
        obs_copies.append(copy)

    up = [
        pltpu.make_async_remote_copy(
            src_ref=notes.at[f, r, t], dst_ref=notes.at[f, r, t], send_sem=send_sem.at[number],
            recv_sem=recv_sem.at[number], device_id=target, device_id_type=MESH,
        )
        for number, target in enumerate(column)
    ]
    for copy in up:
        copy.start()

    for load in loads[3:]:
        load.wait()

    row = lax.broadcasted_iota(jnp.int32, (steps, 1), 0)
    power = row.astype(F32)
    turned = power * angle_in[...]
    grown = jnp.exp(power * jnp.log(decay_in[...]))
    cosine, sine = jnp.cos(turned), jnp.sin(turned)
    half = angle_in.shape[1]
    noise_u = jnp.where(row == 0, 1.0, 1.0 / prec_in[:, :half])
    noise_v = jnp.where(row == 0, 1.0, 1.0 / prec_in[:, half:])
    back = 1.0 / (grown * grown)
    table_ref[0] = grown * cosine
    table_ref[1] = grown * sine
    table_ref[2] = back * (cosine * cosine * noise_u + sine * sine * noise_v)
    table_ref[3] = back * (cosine * sine * (noise_v - noise_u))
    table_ref[4] = back * (sine * sine * noise_u + cosine * cosine * noise_v)
    pick_ref[...] = jnp.broadcast_to((row == position).astype(F32), pick_ref.shape)

    def keep(fibre):
        here = pl.ds(pl.multiple_of(fibre * channels, channels), channels)
        whole = shapes[fibre]
        high_ref[here, :], low_ref[here, :] = split(whole)
        high_t_ref[:, here], low_t_ref[:, here] = split(whole.T)

    keep(f)

    for copy in up:
        copy.wait_recv()
    across = [
        pltpu.make_async_remote_copy(
            src_ref=notes.at[f, r], dst_ref=notes.at[f, r], send_sem=plane_send.at[number],
            recv_sem=plane_recv.at[number], device_id=target, device_id_type=MESH,
        )
        for number, target in enumerate(plane)
    ]
    for copy in across:
        copy.start()

    passed = []
    for i in range(1, n_fibre):
        obs_copies[i - 1].wait_recv()
        source = (f + n_fibre - i) % n_fibre
        for j in range(1, n_rep):
            number = (i - 1) * n_rep + j
            copy = pltpu.make_async_remote_copy(
                src_ref=shapes.at[source, mine], dst_ref=shapes.at[source, mine],
                send_sem=die_send.at[number], recv_sem=die_recv.at[number],
                device_id={"tm": t, "fibre": f, "rep": (r + j) % n_rep}, device_id_type=MESH,
            )
            copy.start()
            passed.append(copy)

    for copy in up:
        copy.wait_send()
    for copy in across:
        copy.wait()

    lane = row <= position
    for fibre in range(n_fibre):
        here = slice(fibre * channels, (fibre + 1) * channels)
        for at in range(steps):
            one = notes.at[fibre, at % n_rep, at // n_rep]
            value = one[:, 0:channels]
            if at:
                value += notes[fibre, (at - 1) % n_rep, (at - 1) // n_rep, :, channels : 2 * channels]
            data_ref[at : at + 1, here] = value
            weight_ref[at : at + 1, here] = one[:, 2 * channels :]
    root = jnp.sqrt(weight_ref[0:steps, :])
    measured = data_ref[0:steps, :]
    masked = jnp.where(lane, root, 0.0)
    weight_ref[0:steps, :] = masked
    weight_ref[steps:, :] = root
    data_ref[0:steps, :] = masked * measured
    data_ref[steps:, :] = root * measured

    for copy in passed:
        copy.wait()
    for copy in obs_copies:
        copy.wait_send()
    for i in range(1, n_fibre):
        keep((f + i) % n_fibre)


def running_sum(value, row, reverse):
    steps = value.shape[0]
    stride = 1
    while stride < steps:
        if reverse:
            value = value + jnp.where(row < steps - stride, pltpu.roll(value, steps - stride, 0), 0.0)
        else:
            value = value + jnp.where(row >= stride, pltpu.roll(value, stride, 0), 0.0)
        stride *= 2
    return value


FIRST = 10
CHUNK = 4
MOST = 4000
TARGET = 2.5e-9
STRONG = 64.0


def solve_kernel(high_ref, low_ref, high_t_ref, low_t_ref, data_ref, weight_ref, table_ref, pick_ref, shapes_ref,
                 filtered_ref, smoothed_ref):
    steps = pick_ref.shape[0]
    half = table_ref.shape[2]
    channels = shapes_ref.shape[1]
    row = lax.broadcasted_iota(jnp.int32, (steps, half), 0)
    weight = weight_ref[...]
    data = data_ref[...]
    both = (slice(0, steps), slice(steps, 2 * steps))

    def times(value, high, low):
        top, rest = split(value)
        n = value.shape[0]
        wide = jnp.dot(jnp.concatenate([top, rest], axis=0), high[...], preferred_element_type=F32)
        return wide[:n] + wide[n:] + jnp.dot(top, low[...], preferred_element_type=F32)

    def carried(seen):
        moved = []
        for rows in both:
            u, v = seen[rows, :half], seen[rows, half:]
            cosine, sine = table_ref[0], table_ref[1]
            u, v = cosine * u + sine * v, cosine * v - sine * u
            u, v = running_sum(u, row, True), running_sum(v, row, True)
            u, v = table_ref[2] * u + table_ref[3] * v, table_ref[3] * u + table_ref[4] * v
            u, v = running_sum(u, row, False), running_sum(v, row, False)
            u, v = cosine * u - sine * v, sine * u + cosine * v
            moved.append(jnp.concatenate([u, v], axis=1))
        return jnp.concatenate(moved, axis=0)

    def states(value):
        return carried(times(weight * value, high_ref, low_ref))

    def apply(value):
        return value + weight * times(states(value), high_t_ref, low_t_ref)

    def states_full(value):
        scaled_value = weight * value
        seen = jnp.zeros((2 * steps, 2 * half), F32)
        for fibre in range(shapes_ref.shape[0]):
            own = scaled_value[:, fibre * channels : (fibre + 1) * channels]
            seen += jnp.dot(own, shapes_ref[fibre], precision=HIGHEST, preferred_element_type=F32)
        return carried(seen)

    def apply_full(value):
        moved = states_full(value)
        back = [
            lax.dot_general(moved, shapes_ref[fibre], (((1,), (1,)), ((), ())), precision=HIGHEST,
                            preferred_element_type=F32)
            for fibre in range(shapes_ref.shape[0])
        ]
        return value + weight * jnp.concatenate(back, axis=1)

    def inner(a, b):
        product = a * b
        return [
            jnp.sum(jnp.sum(product[rows], axis=0, keepdims=True), axis=1, keepdims=True) for rows in both
        ]

    def scaled(factors, value):
        return jnp.concatenate([k * value[rows] for k, rows in zip(factors, both)], axis=0)

    def ratio(a, b):
        good = b > 0
        return jnp.where(good, a / jnp.where(good, b, 1.0), 0.0)

    def store(result):
        pick = pick_ref[...]
        filtered_ref[...] = jnp.sum(pick * result[both[0]], axis=0, keepdims=True)
        smoothed_ref[...] = jnp.sum(pick * result[both[1]], axis=0, keepdims=True)

    zeros = jnp.zeros_like(data)
    none = [jnp.zeros((1, 1), F32)] * 2
    answer, left, along, image, second = zeros, data, zeros, zeros, zeros
    before, size, largest = none, none, none
    goal = None
    mapped = apply(data)
    for number in range(FIRST):
        gamma = inner(left, left)
        delta = inner(left, mapped)
        if number == 0:
            goal = [TARGET * g for g in gamma]
        beta = [ratio(g, o) for g, o in zip(gamma, before)]
        size = [d - b * b * s for d, b, s in zip(delta, beta, size)]
        alpha = [ratio(g, s) for g, s in zip(gamma, size)]
        largest = [jnp.maximum(l, ratio(d, g)) for l, d, g in zip(largest, delta, gamma)]
        before = gamma
        along = left + scaled(beta, along)
        image = mapped + scaled(beta, image)
        answer = answer + scaled(alpha, along)
        left = left - scaled(alpha, image)
        if number + 1 < FIRST:
            second = apply(mapped) + scaled(beta, second)
            mapped = mapped - scaled(alpha, second)
    excess = [jnp.maximum(g - o, l - STRONG) for g, o, l in zip(inner(left, left), goal, largest)]
    store(states(answer))

    def behind(left):
        return jnp.max(jnp.maximum(*[g - o for g, o in zip(inner(left, left), goal)]))

    @pl.when(jnp.max(jnp.maximum(*excess)) > 0)
    def _():
        def step(carry):
            answer, left, along, image, before, size = carry
            mapped = apply_full(left)
            gamma = inner(left, left)
            delta = inner(left, mapped)
            beta = [ratio(g, o) for g, o in zip(gamma, before)]
            size = [d - b * b * s for d, b, s in zip(delta, beta, size)]
            alpha = [ratio(g, s) for g, s in zip(gamma, size)]
            along = left + scaled(beta, along)
            image = mapped + scaled(beta, image)
            return answer + scaled(alpha, along), left - scaled(alpha, image), along, image, gamma, size

        def burst(state):
            count, carry, _ = state
            for _ in range(CHUNK):
                carry = step(carry)
            return count + CHUNK, carry, behind(carry[1])

        def going(state):
            return (state[2] > 0) & (state[0] < MOST)

        start = data - apply_full(answer)
        carry = (answer, start, zeros, zeros, none, none)
        _, carry, _ = lax.while_loop(going, burst, (jnp.int32(0), carry, behind(start)))
        store(states_full(carry[0]))


def solution(mesh):
    counts = tuple(mesh.shape[name] for name in ("tm", "fibre", "rep"))
    steps = counts[0] * counts[2]

    def on_device(records, taps, obs_matrix, noise_prec, proc_prec, mode_decay, mode_angle):
        own, state = obs_matrix.shape
        channels = own * counts[1]
        vmem = pl.BlockSpec(memory_space=pltpu.VMEM)
        hbm = pl.BlockSpec(memory_space=pltpu.HBM)
        shape = jax.ShapeDtypeStruct
        hop, width = records.shape[1], taps.shape[1]
        parts = pl.pallas_call(
            functools.partial(gather_kernel, counts),
            out_shape=(
                shape((channels, state), BF16), shape((channels, state), BF16),
                shape((state, channels), BF16), shape((state, channels), BF16),
                shape((2 * steps, channels), F32), shape((2 * steps, channels), F32),
                shape((5, steps, state // 2), F32), shape((steps, state), F32),
                shape((counts[1], own, state), F32),
            ),
            in_specs=[hbm] * 7,
            out_specs=(vmem,) * 9,
            scratch_shapes=[
                pltpu.VMEM((hop, own), BF16),
                pltpu.VMEM((width, own), F32),
                pltpu.VMEM((1, own), F32),
                pltpu.VMEM((1, state), F32),
                pltpu.VMEM((1, state // 2), F32),
                pltpu.VMEM((1, state // 2), F32),
                pltpu.VMEM((counts[1], counts[2], counts[0], 1, 3 * own), F32),
                pltpu.SemaphoreType.DMA((7,)),
                pltpu.SemaphoreType.DMA((counts[0],)),
                pltpu.SemaphoreType.DMA((counts[0],)),
                pltpu.SemaphoreType.DMA((counts[1] * counts[2],)),
                pltpu.SemaphoreType.DMA((counts[1] * counts[2],)),
                pltpu.SemaphoreType.DMA((counts[1],)),
                pltpu.SemaphoreType.DMA((counts[1],)),
                pltpu.SemaphoreType.DMA((counts[1] * counts[2],)),
                pltpu.SemaphoreType.DMA((counts[1] * counts[2],)),
            ],
            compiler_params=pltpu.CompilerParams(
                collective_id=0, has_side_effects=True, vmem_limit_bytes=32 * 2**20
            ),
        )(*(
            pltpu.with_memory_space_constraint(value, pltpu.HBM)
            for value in (
                records.T, taps.T, obs_matrix, noise_prec, proc_prec[None], mode_decay[None], mode_angle[None]
            )
        ))
        return pl.pallas_call(
            solve_kernel,
            out_shape=(shape((1, state), F32), shape((1, state), F32)),
            in_specs=[vmem] * 9,
            out_specs=(vmem, vmem),
            compiler_params=pltpu.CompilerParams(vmem_limit_bytes=32 * 2**20),
        )(*parts)

    return jax.shard_map(
        on_device,
        mesh=mesh,
        in_specs=(
            P(("grp", "fibre"), ("tm", "rep")),
            P("fibre", None),
            P("fibre", None),
            P(("grp", "tm", "rep"), "fibre"),
            P(),
            P(),
            P(),
        ),
        out_specs=(P(("grp", "tm", "rep"), None), P(("grp", "tm", "rep"), None)),
        check_vma=False,
    )
```

```python
import functools

import jax
import jax.numpy as jnp
from jax import lax
from jax.experimental import pallas as pl
from jax.experimental.pallas import tpu as pltpu
from jax.sharding import PartitionSpec as P

F32 = jnp.float32
BF16 = jnp.bfloat16
MESH = pl.DeviceIdType.MESH
HIGHEST = lax.Precision.HIGHEST


def split(value):
    high = value.astype(BF16)
    return high, (value - high.astype(F32)).astype(BF16)


def gather_kernel(
    counts, records_ref, taps_ref, obs_ref, noise_ref, prec_ref, decay_ref, angle_ref,
    high_ref, low_ref, high_t_ref, low_t_ref, data_ref, weight_ref, table_ref, pick_ref, shapes,
    records_in, taps_in, noise_in, prec_in, decay_in, angle_in,
    notes, local_sem, send_sem, recv_sem, plane_send, plane_recv, obs_send, obs_recv, die_send, die_recv,
):
    n_tm, n_fibre, n_rep = counts
    steps = n_tm * n_rep
    channels = obs_ref.shape[0]
    t, f, r = lax.axis_index("tm"), lax.axis_index("fibre"), lax.axis_index("rep")
    position = t * n_rep + r
    column = [{"tm": (t + i) % n_tm, "fibre": f, "rep": r} for i in range(1, n_tm)]
    plane = [
        {"tm": t, "fibre": (f + i) % n_fibre, "rep": (r + j) % n_rep}
        for i in range(n_fibre) for j in range(n_rep) if i or j
    ]
    barrier = pltpu.get_barrier_semaphore()
    for target in plane + column:
        pl.semaphore_signal(barrier, inc=1, device_id=target, device_id_type=MESH)

    loads = [
        pltpu.make_async_copy(source, target, local_sem.at[number])
        for number, (source, target) in enumerate((
            (records_ref, records_in), (taps_ref, taps_in), (noise_ref, noise_in), (prec_ref, prec_in),
            (decay_ref, decay_in), (angle_ref, angle_in), (obs_ref, shapes.at[f]),
        ))
    ]
    for load in loads:
        load.start()
    for load in loads[:3]:
        load.wait()

    block = records_in[...].astype(F32)
    hop = block.shape[0]
    mine_note = notes.at[f, r, t]
    mine_note[:, 0:channels] = jnp.sum(block * taps_in[hop:, :], axis=0, keepdims=True)
    mine_note[:, channels : 2 * channels] = jnp.sum(block * taps_in[:hop, :], axis=0, keepdims=True)
    mine_note[:, 2 * channels :] = noise_in[...]

    pl.semaphore_wait(barrier, len(column) + len(plane))

    share = channels // n_rep
    mine = pl.ds(pl.multiple_of(r * share, share), share)
    obs_copies = []
    for i in range(1, n_fibre):
        copy = pltpu.make_async_remote_copy(
            src_ref=obs_ref.at[mine], dst_ref=shapes.at[f, mine], send_sem=obs_send.at[i], recv_sem=obs_recv.at[i],
            device_id={"tm": t, "fibre": (f + i) % n_fibre, "rep": r}, device_id_type=MESH,
        )
        copy.start()
        obs_copies.append(copy)

    up = [
        pltpu.make_async_remote_copy(
            src_ref=notes.at[f, r, t], dst_ref=notes.at[f, r, t], send_sem=send_sem.at[number],
            recv_sem=recv_sem.at[number], device_id=target, device_id_type=MESH,
        )
        for number, target in enumerate(column)
    ]
    for copy in up:
        copy.start()

    for load in loads[3:]:
        load.wait()

    row = lax.broadcasted_iota(jnp.int32, (steps, 1), 0)
    power = row.astype(F32)
    turned = power * angle_in[...]
    grown = jnp.exp(power * jnp.log(decay_in[...]))
    cosine, sine = jnp.cos(turned), jnp.sin(turned)
    half = angle_in.shape[1]
    noise_u = jnp.where(row == 0, 1.0, 1.0 / prec_in[:, :half])
    noise_v = jnp.where(row == 0, 1.0, 1.0 / prec_in[:, half:])
    back = 1.0 / (grown * grown)
    table_ref[0] = grown * cosine
    table_ref[1] = grown * sine
    table_ref[2] = back * (cosine * cosine * noise_u + sine * sine * noise_v)
    table_ref[3] = back * (cosine * sine * (noise_v - noise_u))
    table_ref[4] = back * (sine * sine * noise_u + cosine * cosine * noise_v)
    pick_ref[...] = jnp.broadcast_to((row == position).astype(F32), pick_ref.shape)

    def keep(fibre):
        here = pl.ds(pl.multiple_of(fibre * channels, channels), channels)
        whole = shapes[fibre]
        high_ref[here, :], low_ref[here, :] = split(whole)
        high_t_ref[:, here], low_t_ref[:, here] = split(whole.T)

    keep(f)

    for copy in up:
        copy.wait_recv()
    across = [
        pltpu.make_async_remote_copy(
            src_ref=notes.at[f, r], dst_ref=notes.at[f, r], send_sem=plane_send.at[number],
            recv_sem=plane_recv.at[number], device_id=target, device_id_type=MESH,
        )
        for number, target in enumerate(plane)
    ]
    for copy in across:
        copy.start()

    passed = []
    for i in range(1, n_fibre):
        obs_copies[i - 1].wait_recv()
        source = (f + n_fibre - i) % n_fibre
        for j in range(1, n_rep):
            number = (i - 1) * n_rep + j
            copy = pltpu.make_async_remote_copy(
                src_ref=shapes.at[source, mine], dst_ref=shapes.at[source, mine],
                send_sem=die_send.at[number], recv_sem=die_recv.at[number],
                device_id={"tm": t, "fibre": f, "rep": (r + j) % n_rep}, device_id_type=MESH,
            )
            copy.start()
            passed.append(copy)

    for copy in up:
        copy.wait_send()
    for copy in across:
        copy.wait()

    lane = row <= position
    for fibre in range(n_fibre):
        here = slice(fibre * channels, (fibre + 1) * channels)
        for at in range(steps):
            one = notes.at[fibre, at % n_rep, at // n_rep]
            value = one[:, 0:channels]
            if at:
                value += notes[fibre, (at - 1) % n_rep, (at - 1) // n_rep, :, channels : 2 * channels]
            data_ref[at : at + 1, here] = value
            weight_ref[at : at + 1, here] = one[:, 2 * channels :]
    root = jnp.sqrt(weight_ref[0:steps, :])
    measured = data_ref[0:steps, :]
    masked = jnp.where(lane, root, 0.0)
    weight_ref[0:steps, :] = masked
    weight_ref[steps:, :] = root
    data_ref[0:steps, :] = masked * measured
    data_ref[steps:, :] = root * measured

    for copy in passed:
        copy.wait()
    for copy in obs_copies:
        copy.wait_send()
    for i in range(1, n_fibre):
        keep((f + i) % n_fibre)


def running_sum(value, row, reverse):
    steps = value.shape[0]
    stride = 1
    while stride < steps:
        if reverse:
            value = value + jnp.where(row < steps - stride, pltpu.roll(value, steps - stride, 0), 0.0)
        else:
            value = value + jnp.where(row >= stride, pltpu.roll(value, stride, 0), 0.0)
        stride *= 2
    return value


FIRST = 10
CHUNK = 4
MOST = 4000
TARGET = 2.5e-9
STRONG = 64.0


def solve_kernel(high_ref, low_ref, high_t_ref, low_t_ref, data_ref, weight_ref, table_ref, pick_ref, shapes_ref,
                 filtered_ref, smoothed_ref):
    steps = pick_ref.shape[0]
    half = table_ref.shape[2]
    channels = shapes_ref.shape[1]
    row = lax.broadcasted_iota(jnp.int32, (steps, half), 0)
    weight = weight_ref[...]
    data = data_ref[...]
    both = (slice(0, steps), slice(steps, 2 * steps))

    def times(value, high, low):
        top, rest = split(value)
        n = value.shape[0]
        wide = jnp.dot(jnp.concatenate([top, rest], axis=0), high[...], preferred_element_type=F32)
        return wide[:n] + wide[n:] + jnp.dot(top, low[...], preferred_element_type=F32)

    def carried(seen):
        moved = []
        for rows in both:
            u, v = seen[rows, :half], seen[rows, half:]
            cosine, sine = table_ref[0], table_ref[1]
            u, v = cosine * u + sine * v, cosine * v - sine * u
            u, v = running_sum(u, row, True), running_sum(v, row, True)
            u, v = table_ref[2] * u + table_ref[3] * v, table_ref[3] * u + table_ref[4] * v
            u, v = running_sum(u, row, False), running_sum(v, row, False)
            u, v = cosine * u - sine * v, sine * u + cosine * v
            moved.append(jnp.concatenate([u, v], axis=1))
        return jnp.concatenate(moved, axis=0)

    def states(value):
        return carried(times(weight * value, high_ref, low_ref))

    def apply(value):
        return value + weight * times(states(value), high_t_ref, low_t_ref)

    def states_full(value):
        scaled_value = weight * value
        seen = jnp.zeros((2 * steps, 2 * half), F32)
        for fibre in range(shapes_ref.shape[0]):
            own = scaled_value[:, fibre * channels : (fibre + 1) * channels]
            seen += jnp.dot(own, shapes_ref[fibre], precision=HIGHEST, preferred_element_type=F32)
        return carried(seen)

    def apply_full(value):
        moved = states_full(value)
        back = [
            lax.dot_general(moved, shapes_ref[fibre], (((1,), (1,)), ((), ())), precision=HIGHEST,
                            preferred_element_type=F32)
            for fibre in range(shapes_ref.shape[0])
        ]
        return value + weight * jnp.concatenate(back, axis=1)

    def inner(a, b):
        product = a * b
        return [
            jnp.sum(jnp.sum(product[rows], axis=0, keepdims=True), axis=1, keepdims=True) for rows in both
        ]

    def scaled(factors, value):
        return jnp.concatenate([k * value[rows] for k, rows in zip(factors, both)], axis=0)

    def ratio(a, b):
        good = b > 0
        return jnp.where(good, a / jnp.where(good, b, 1.0), 0.0)

    def store(result):
        pick = pick_ref[...]
        filtered_ref[...] = jnp.sum(pick * result[both[0]], axis=0, keepdims=True)
        smoothed_ref[...] = jnp.sum(pick * result[both[1]], axis=0, keepdims=True)

    zeros = jnp.zeros_like(data)
    none = [jnp.zeros((1, 1), F32)] * 2
    answer, left, along, image, second = zeros, data, zeros, zeros, zeros
    before, size, largest = none, none, none
    goal = None
    mapped = apply(data)
    for number in range(FIRST):
        gamma = inner(left, left)
        delta = inner(left, mapped)
        if number == 0:
            goal = [TARGET * g for g in gamma]
        beta = [ratio(g, o) for g, o in zip(gamma, before)]
        size = [d - b * b * s for d, b, s in zip(delta, beta, size)]
        alpha = [ratio(g, s) for g, s in zip(gamma, size)]
        largest = [jnp.maximum(l, ratio(d, g)) for l, d, g in zip(largest, delta, gamma)]
        before = gamma
        along = left + scaled(beta, along)
        image = mapped + scaled(beta, image)
        answer = answer + scaled(alpha, along)
        left = left - scaled(alpha, image)
        if number + 1 < FIRST:
            second = apply(mapped) + scaled(beta, second)
            mapped = mapped - scaled(alpha, second)
    excess = [jnp.maximum(g - o, l - STRONG) for g, o, l in zip(inner(left, left), goal, largest)]
    store(states(answer))

    def behind(left):
        return jnp.max(jnp.maximum(*[g - o for g, o in zip(inner(left, left), goal)]))

    @pl.when(jnp.max(jnp.maximum(*excess)) > 0)
    def _():
        def step(carry):
            answer, left, along, image, before, size = carry
            mapped = apply_full(left)
            gamma = inner(left, left)
            delta = inner(left, mapped)
            beta = [ratio(g, o) for g, o in zip(gamma, before)]
            size = [d - b * b * s for d, b, s in zip(delta, beta, size)]
            alpha = [ratio(g, s) for g, s in zip(gamma, size)]
            along = left + scaled(beta, along)
            image = mapped + scaled(beta, image)
            return answer + scaled(alpha, along), left - scaled(alpha, image), along, image, gamma, size

        def burst(state):
            count, carry, _ = state
            for _ in range(CHUNK):
                carry = step(carry)
            return count + CHUNK, carry, behind(carry[1])

        def going(state):
            return (state[2] > 0) & (state[0] < MOST)

        start = data - apply_full(answer)
        carry = (answer, start, zeros, zeros, none, none)
        _, carry, _ = lax.while_loop(going, burst, (jnp.int32(0), carry, behind(start)))
        store(states_full(carry[0]))


def solution(mesh):
    counts = tuple(mesh.shape[name] for name in ("tm", "fibre", "rep"))
    steps = counts[0] * counts[2]

    def on_device(records, taps, obs_matrix, noise_prec, proc_prec, mode_decay, mode_angle):
        own, state = obs_matrix.shape
        channels = own * counts[1]
        vmem = pl.BlockSpec(memory_space=pltpu.VMEM)
        hbm = pl.BlockSpec(memory_space=pltpu.HBM)
        shape = jax.ShapeDtypeStruct
        hop, width = records.shape[1], taps.shape[1]
        parts = pl.pallas_call(
            functools.partial(gather_kernel, counts),
            out_shape=(
                shape((channels, state), BF16), shape((channels, state), BF16),
                shape((state, channels), BF16), shape((state, channels), BF16),
                shape((2 * steps, channels), F32), shape((2 * steps, channels), F32),
                shape((5, steps, state // 2), F32), shape((steps, state), F32),
                shape((counts[1], own, state), F32),
            ),
            in_specs=[hbm] * 7,
            out_specs=(vmem,) * 9,
            scratch_shapes=[
                pltpu.VMEM((hop, own), BF16),
                pltpu.VMEM((width, own), F32),
                pltpu.VMEM((1, own), F32),
                pltpu.VMEM((1, state), F32),
                pltpu.VMEM((1, state // 2), F32),
                pltpu.VMEM((1, state // 2), F32),
                pltpu.VMEM((counts[1], counts[2], counts[0], 1, 3 * own), F32),
                pltpu.SemaphoreType.DMA((7,)),
                pltpu.SemaphoreType.DMA((counts[0],)),
                pltpu.SemaphoreType.DMA((counts[0],)),
                pltpu.SemaphoreType.DMA((counts[1] * counts[2],)),
                pltpu.SemaphoreType.DMA((counts[1] * counts[2],)),
                pltpu.SemaphoreType.DMA((counts[1],)),
                pltpu.SemaphoreType.DMA((counts[1],)),
                pltpu.SemaphoreType.DMA((counts[1] * counts[2],)),
                pltpu.SemaphoreType.DMA((counts[1] * counts[2],)),
            ],
            compiler_params=pltpu.CompilerParams(
                collective_id=0, has_side_effects=True, vmem_limit_bytes=32 * 2**20
            ),
        )(*(
            pltpu.with_memory_space_constraint(value, pltpu.HBM)
            for value in (
                records.T, taps.T, obs_matrix, noise_prec, proc_prec[None], mode_decay[None], mode_angle[None]
            )
        ))
        return pl.pallas_call(
            solve_kernel,
            out_shape=(shape((1, state), F32), shape((1, state), F32)),
            in_specs=[vmem] * 9,
            out_specs=(vmem, vmem),
            compiler_params=pltpu.CompilerParams(vmem_limit_bytes=32 * 2**20),
        )(*parts)

    return jax.shard_map(
        on_device,
        mesh=mesh,
        in_specs=(
            P(("grp", "fibre"), ("tm", "rep")),
            P("fibre", None),
            P("fibre", None),
            P(("grp", "tm", "rep"), "fibre"),
            P(),
            P(),
            P(),
        ),
        out_specs=(P(("grp", "tm", "rep"), None), P(("grp", "tm", "rep"), None)),
        check_vma=False,
    )
```
